512 devices in a mesh: mx: 16 (over y, core), my: 32 (over x, z).
Axes of the slice: x: 4, y: 8, z: 8, core: 2. Of those that a mesh axis runs over, the one named last changes fastest.
Arguments:
- patches: bfloat16 [256, 6144], P('my', 'mx'), may hold values from -6 to 6
- cotangent: bfloat16 [256, 6144], P('my', 'mx'), may hold values from -0.75 to 0.75
- w_qkv: bfloat16 [6144, 3, 4096], P('mx', None, 'my'), may hold values from -0.078125 to 0.078125
- w_out: bfloat16 [4096, 6144], P('my', 'mx'), may hold values from -0.09375 to 0.09375
- w_up: bfloat16 [6144, 24576], P('mx', 'my'), may hold values from -0.078125 to 0.078125
- w_down: bfloat16 [24576, 6144], P('my', 'mx'), may hold values from -0.0390625 to 0.0390625
- dir_qkv: bfloat16 [6144, 3, 4096], P('mx', None, 'my'), may hold values from -0.078125 to 0.078125
- dir_out: bfloat16 [4096, 6144], P('my', 'mx'), may hold values from -0.09375 to 0.09375
- dir_up: bfloat16 [6144, 24576], P('mx', 'my'), may hold values from -0.078125 to 0.078125
- dir_down: bfloat16 [24576, 6144], P('my', 'mx'), may hold values from -0.0390625 to 0.0390625
Outputs:
- hvp_qkv: bfloat16 [6144, 3, 4096], P('mx', None, 'my')
- hvp_out: bfloat16 [4096, 6144], P('my', 'mx')
- hvp_up: bfloat16 [6144, 24576], P('mx', 'my')
- hvp_down: bfloat16 [24576, 6144], P('my', 'mx')
The draws below stay inside these ranges and needn't reach their ends.
All inputs are finite; a program needn't handle non-finite values.
Results may differ from the reference program's by a relative error of at most 0.0049.
Values may be sent and summed in bfloat16 or wider, within the bound.
No kernel may reach another device: no remote copies, remote signals or barrier semaphores. Data moves between devices by JAX's collectives and lax.ppermute only.
A program may use at most 64 MiB of HBM per device.

```python
import math
import jax
import jax.numpy as jnp
from jax import lax

D = 6144
FF = 24576
HD = 128
HEADS = 32
PATCHES = 256


def block_levels(own_key, dims, cuts, smallest, high):
    loudness = 1.0
    for axis_at, blocks in cuts:
        heights = jax.random.uniform(jax.random.fold_in(jax.random.fold_in(own_key, 6), axis_at), (blocks,), jnp.float32, smallest / len(cuts), high / len(cuts))
        loudness = loudness * jnp.repeat(jnp.exp(heights), dims[axis_at] // blocks).reshape((-1,) + (1,) * (len(dims) - 1 - axis_at))
    return loudness


def scatter_about(key, shape, deviation, bound, cuts=(), held_as=jnp.bfloat16):
    loudness = block_levels(key, shape, cuts, -0.22, 0.18) if cuts else 1.0
    entries = jax.random.normal(key, shape, jnp.float32) * deviation * loudness
    return jnp.minimum(jnp.maximum(entries, -bound), bound).astype(held_as)


def setup_inputs(seed: int = 0) -> dict:
    seeds = jax.random.split(jax.random.key(seed), 11)
    patches = scatter_about(seeds[0], (PATCHES, D), 1.0, 6.0, ((0, 32), (1, 16)))
    cotangent = scatter_about(seeds[1], (PATCHES, D), 0.125, 0.75, ((0, 32), (1, 16)))
    w_qkv = scatter_about(seeds[2], (D, 3, HEADS * HD), D ** -0.5, 0.078125, ((0, 16), (2, 32)))
    w_out = scatter_about(seeds[3], (HEADS * HD, D), (HEADS * HD) ** -0.5, 0.09375, ((0, 32), (1, 16)))
    w_up = scatter_about(seeds[4], (D, FF), D ** -0.5, 0.078125, ((0, 16), (1, 32)))
    w_down = scatter_about(seeds[5], (FF, D), FF ** -0.5, 0.0390625, ((0, 32), (1, 16)))
    dir_qkv = scatter_about(seeds[6], (D, 3, HEADS * HD), D ** -0.5, 0.078125, ((0, 16), (2, 32)))
    dir_out = scatter_about(seeds[7], (HEADS * HD, D), (HEADS * HD) ** -0.5, 0.09375, ((0, 32), (1, 16)))
    dir_up = scatter_about(seeds[8], (D, FF), D ** -0.5, 0.078125, ((0, 16), (1, 32)))
    dir_down = scatter_about(seeds[9], (FF, D), FF ** -0.5, 0.0390625, ((0, 32), (1, 16)))
    return dict(patches=patches, cotangent=cotangent, w_qkv=w_qkv, w_out=w_out, w_up=w_up, w_down=w_down, dir_qkv=dir_qkv, dir_out=dir_out, dir_up=dir_up, dir_down=dir_down)


def normalize(block):
    centered = block - lax.optimization_barrier(jnp.mean(block, axis=-1, keepdims=True))
    return centered / jnp.sqrt(lax.optimization_barrier(jnp.mean(centered * centered, axis=-1, keepdims=True)) + 1e-06)

def attend(pre):
    count = pre.shape[0]
    heads = pre.shape[2] // HD
    parts = pre.reshape(count, 3, heads, HD)
    query = normalize(parts[:, 0])
    keys = normalize(parts[:, 1])
    values = parts[:, 2]
    scores = jnp.einsum('phd,khd->hpk', query, keys, precision=lax.Precision.HIGHEST) / math.sqrt(HD)
    raised = jnp.exp(scores)
    probs = raised / lax.optimization_barrier(jnp.sum(raised, axis=2, keepdims=True))
    mixed = jnp.einsum('hpk,khd->phd', probs, values, precision=lax.Precision.HIGHEST)
    return mixed.reshape(count, heads * HD)

def attention_pair(pre, cot_in):
    result, pull = jax.vjp(attend, pre)
    return (result, pull(cot_in)[0])

def hidden_pair(pre, cot_in):
    result, pull = jax.vjp(jax.nn.gelu, pre)
    return (result, pull(cot_in)[0])

def reference(patches, cotangent, w_qkv, w_out, w_up, w_down, dir_qkv, dir_out, dir_up, dir_down):
    width = w_qkv.shape[0]
    span = w_qkv.shape[2]
    count = patches.shape[0]
    pre_qkv = jnp.dot(patches, w_qkv.reshape(width, 3 * span), preferred_element_type=jnp.float32).reshape(count, 3, span)
    tan_qkv = jnp.dot(patches, dir_qkv.reshape(width, 3 * span), preferred_element_type=jnp.float32).reshape(count, 3, span)
    pre_hidden = jnp.dot(patches, w_up, preferred_element_type=jnp.float32)
    tan_hidden = jnp.dot(patches, dir_up, preferred_element_type=jnp.float32)
    cot_mixed = jnp.dot(cotangent, w_out.T, preferred_element_type=jnp.float32)
    tan_mixed = jnp.dot(cotangent, dir_out.T, preferred_element_type=jnp.float32)
    cot_act = jnp.dot(cotangent, w_down.T, preferred_element_type=jnp.float32)
    tan_act = jnp.dot(cotangent, dir_down.T, preferred_element_type=jnp.float32)
    attn_tan = jax.jvp(attention_pair, (pre_qkv, cot_mixed), (tan_qkv, tan_mixed))[1]
    hid_tan = jax.jvp(hidden_pair, (pre_hidden, cot_act), (tan_hidden, tan_act))[1]
    mixed_low = attn_tan[0].astype(jnp.bfloat16)
    pre_low = attn_tan[1].reshape(count, 3 * span).astype(jnp.bfloat16)
    act_low = hid_tan[0].astype(jnp.bfloat16)
    hid_low = hid_tan[1].astype(jnp.bfloat16)
    hvp_qkv = jnp.dot(patches.T, pre_low, preferred_element_type=jnp.float32).reshape(width, 3, span).astype(jnp.bfloat16)
    hvp_out = jnp.dot(mixed_low.T, cotangent, preferred_element_type=jnp.float32).astype(jnp.bfloat16)
    hvp_up = jnp.dot(patches.T, hid_low, preferred_element_type=jnp.float32).astype(jnp.bfloat16)
    hvp_down = jnp.dot(act_low.T, cotangent, preferred_element_type=jnp.float32).astype(jnp.bfloat16)
    return (hvp_qkv, hvp_out, hvp_up, hvp_down)
```

```python
import math

import jax
import jax.numpy as jnp
from jax import lax
from jax.sharding import PartitionSpec as P

HD = 128


def normalize(block):
    centered = block - jnp.mean(block, axis=-1, keepdims=True)
    return centered / jnp.sqrt(jnp.mean(centered * centered, axis=-1, keepdims=True) + 1e-06)


def attend(pre):
    count = pre.shape[0]
    heads = pre.shape[2] // HD
    parts = pre.reshape(count, 3, heads, HD)
    query = normalize(parts[:, 0])
    keys = normalize(parts[:, 1])
    values = parts[:, 2]
    scores = jnp.einsum("phd,khd->hpk", query, keys, precision=lax.Precision.HIGHEST) / math.sqrt(
        HD
    )
    raised = jnp.exp(scores)
    probs = raised / jnp.sum(raised, axis=2, keepdims=True)
    mixed = jnp.einsum("hpk,khd->phd", probs, values, precision=lax.Precision.HIGHEST)
    return mixed.reshape(count, heads * HD)


def attention_pair(pre, cot_in):
    result, pull = jax.vjp(attend, pre)
    return (result, pull(cot_in)[0])


def hidden_pair(pre, cot_in):
    result, pull = jax.vjp(jax.nn.gelu, pre)
    return (result, pull(cot_in)[0])


def project(left, right):
    return jnp.dot(left, right, preferred_element_type=jnp.float32)


def project_back(left, right):
    return jnp.einsum("pd,ed->pe", left, right, preferred_element_type=jnp.float32)


def spread(exponents):
    return jnp.repeat(exponents, HD, axis=-1)


def pack(block, exponents):
    rows = block.shape[0]
    scaled = block * jnp.exp2(14.0 - spread(exponents))
    tail = jnp.broadcast_to(jnp.pad(exponents, (0, HD - 8)), (rows, HD))
    return jnp.concatenate([scaled, tail], axis=1).astype(jnp.float16)


def unpack(message):
    wide = message.astype(jnp.float32)
    exponents = wide[..., 8 * HD : 8 * HD + 8]
    return wide[..., : 8 * HD] * jnp.exp2(spread(exponents) - 14.0), exponents


def body(patches, cotangent, w_qkv, w_out, w_up, w_down, dir_qkv, dir_out, dir_up, dir_down):
    wide = lax.axis_size("mx")
    long = lax.axis_size("my")
    chips = wide // 2
    core = lax.rem(lax.axis_index("mx"), 2)
    ring = [[chip * 2 + c for chip in range(chips)] for c in range(2)]
    swap = [(i, i ^ 1) for i in range(wide)]
    width = w_qkv.shape[0]
    span = w_qkv.shape[2]
    own_rows = patches.shape[0]
    count = own_rows * long
    half = count // 2
    share = half // chips

    both = jnp.stack([patches, cotangent])
    gathered = lax.all_to_all(
        jnp.broadcast_to(both, (long,) + both.shape), "my", 0, 0, tiled=True
    )
    rows_all = gathered[:, 0].reshape(count, width)
    cot_all = gathered[:, 1].reshape(count, width)
    own = lambda a: lax.dynamic_slice_in_dim(a, core * half, half, 0)
    other = lambda a: lax.dynamic_slice_in_dim(a, (1 - core) * half, half, 0)
    rows_all = jnp.concatenate([own(rows_all), other(rows_all)])
    cot_all = jnp.concatenate([own(cot_all), other(cot_all)])

    attn_part = jnp.concatenate(
        [
            project(rows_all, w_qkv.reshape(width, 3 * span)),
            project(rows_all, dir_qkv.reshape(width, 3 * span)),
            project_back(cot_all, w_out),
            project_back(cot_all, dir_out),
        ],
        axis=1,
    )
    hid_part = jnp.concatenate(
        [
            project(rows_all, w_up),
            project(rows_all, dir_up),
            project_back(cot_all, w_down),
            project_back(cot_all, dir_down),
        ],
        axis=1,
    )
    attn_sum = attn_part[:half] + lax.ppermute(attn_part[half:], "mx", swap)
    hid_sum = hid_part[:half] + lax.ppermute(hid_part[half:], "mx", swap)

    top = jnp.max(jnp.abs(attn_sum).reshape(half, 8, HD), axis=(0, 2))
    exponents = jnp.clip(jnp.ceil(jnp.log2(top)), -100.0, 100.0)
    message = pack(attn_sum, exponents).reshape(chips, share, 9 * HD)
    attn_parts, came = unpack(
        lax.all_to_all(message, "mx", 0, 0, tiled=True, axis_index_groups=ring)
    )
    hid_parts = lax.all_to_all(
        hid_sum.astype(jnp.bfloat16).reshape(chips, share, -1),
        "mx",
        0,
        0,
        tiled=True,
        axis_index_groups=ring,
    )
    attn_rows = pack(jnp.sum(attn_parts, axis=0), jnp.max(came, axis=(0, 1)) + 3.0)
    attn_half = lax.all_to_all(
        jnp.broadcast_to(attn_rows, (chips,) + attn_rows.shape),
        "mx",
        0,
        0,
        tiled=True,
        axis_index_groups=ring,
    ).reshape(half, 9 * HD)
    attn_all = unpack(
        jnp.concatenate([attn_half, lax.ppermute(attn_half, "mx", swap)])
    )[0]

    hidden = jnp.sum(hid_parts.astype(jnp.float32), axis=0)
    pre_hidden, tan_hidden, cot_act, tan_act = jnp.split(hidden, 4, axis=1)
    hid_tan = jax.jvp(hidden_pair, (pre_hidden, cot_act), (tan_hidden, tan_act))[1]
    lows = jnp.concatenate(
        [hid_tan[0].astype(jnp.bfloat16), hid_tan[1].astype(jnp.bfloat16)], axis=1
    )
    low_half = lax.all_to_all(
        jnp.broadcast_to(lows, (chips,) + lows.shape),
        "mx",
        0,
        0,
        tiled=True,
        axis_index_groups=ring,
    ).reshape(half, -1)
    low_all = jnp.concatenate([low_half, lax.ppermute(low_half, "mx", swap)])
    act_low, hid_low = jnp.split(low_all, 2, axis=1)

    pre_qkv = attn_all[:, : 3 * HD].reshape(count, 3, span)
    tan_qkv = attn_all[:, 3 * HD : 6 * HD].reshape(count, 3, span)
    cot_mixed = attn_all[:, 6 * HD : 7 * HD]
    tan_mixed = attn_all[:, 7 * HD : 8 * HD]
    attn_tan = jax.jvp(attention_pair, (pre_qkv, cot_mixed), (tan_qkv, tan_mixed))[1]
    mixed_low = attn_tan[0].astype(jnp.bfloat16)
    pre_low = attn_tan[1].reshape(count, 3 * span).astype(jnp.bfloat16)
    hvp_qkv = jnp.einsum("pd,pe->de", rows_all, pre_low, preferred_element_type=jnp.float32)
    hvp_out = jnp.einsum("pe,pd->ed", mixed_low, cot_all, preferred_element_type=jnp.float32)
    hvp_up = jnp.einsum("pd,pe->de", rows_all, hid_low, preferred_element_type=jnp.float32)
    hvp_down = jnp.einsum("pe,pd->ed", act_low, cot_all, preferred_element_type=jnp.float32)
    return (
        hvp_qkv.reshape(width, 3, span).astype(jnp.bfloat16),
        hvp_out.astype(jnp.bfloat16),
        hvp_up.astype(jnp.bfloat16),
        hvp_down.astype(jnp.bfloat16),
    )


def solution(mesh):
    return jax.shard_map(
        body,
        mesh=mesh,
        in_specs=(
            P("my", "mx"),
            P("my", "mx"),
            P("mx", None, "my"),
            P("my", "mx"),
            P("mx", "my"),
            P("my", "mx"),
            P("mx", None, "my"),
            P("my", "mx"),
            P("mx", "my"),
            P("my", "mx"),
        ),
        out_specs=(P("mx", None, "my"), P("my", "mx"), P("mx", "my"), P("my", "mx")),
        check_vma=False,
    )
```

```python
import math

import jax
import jax.numpy as jnp
from jax import lax
from jax.experimental import pallas as pl
from jax.experimental.pallas import tpu as pltpu
from jax.sharding import PartitionSpec as P

HD = 128
F32 = jnp.float32
BF16 = jnp.bfloat16
VMEM = pl.BlockSpec(memory_space=pltpu.VMEM)
SMEM = pl.BlockSpec(memory_space=pltpu.SMEM)

NN = ((1,), (0,))
NT = ((1,), (1,))
TN = ((0,), (0,))


def dot(left, right, dims):
    return lax.dot_general(left, right, (dims, ((), ())), preferred_element_type=F32)


def halves(x):
    high = x.astype(BF16)
    return high, (x - high.astype(F32)).astype(BF16)


def dot3(left, right, dims):
    return (
        dot(left[0], right[0], dims) + dot(left[0], right[1], dims) + dot(left[1], right[0], dims)
    )


def mean(x):
    return jnp.mean(x, axis=-1, keepdims=True)


def total(x):
    return jnp.sum(x, axis=-1, keepdims=True)


def centre(x):
    return x - mean(x)


def normalize(x, x_tan):
    centred = centre(x)
    inverse = lax.rsqrt(mean(centred * centred) + 1e-06)
    y = centred * inverse
    shift = mean(y * x_tan)
    return y, (centre(x_tan) - y * shift) * inverse, inverse, shift


def normalize_back(y, y_tan, inverse, shift, cot, cot_tan):
    along = mean(y * cot)
    back = (centre(cot) - y * along) * inverse
    along_tan = mean(y_tan * cot) + mean(y * cot_tan)
    return (centre(cot_tan) - y_tan * along - y * along_tan - back * shift) * inverse


def attention(q, k, v, tq, tk, tv, cot, cot_tan):
    scale = 1.0 / math.sqrt(HD)
    qn, dqn, q_inverse, q_shift = normalize(q, tq)
    kn, dkn, k_inverse, k_shift = normalize(k, tk)
    qs, dqs, ks, dks = halves(qn * scale), halves(dqn * scale), halves(kn), halves(dkn)
    vs, dvs, cs, dcs = halves(v), halves(tv), halves(cot), halves(cot_tan)
    raised = jnp.exp(dot3(qs, ks, NT))
    probs = raised / total(raised)
    score_tan = dot3(dqs, ks, NT) + dot3(qs, dks, NT)
    probs_tan = probs * (score_tan - total(probs * score_tan))
    ps, dps = halves(probs), halves(probs_tan)
    mixed_tan = dot3(dps, vs, NN) + dot3(ps, dvs, NN)
    v_tan = dot3(dps, cs, TN) + dot3(ps, dcs, TN)
    cot_probs = dot3(cs, vs, NT)
    cot_probs_tan = dot3(dcs, vs, NT) + dot3(cs, dvs, NT)
    away = cot_probs - total(probs * cot_probs)
    away_tan = cot_probs_tan - total(probs_tan * cot_probs + probs * cot_probs_tan)
    ss, dss = halves(probs * away), halves(probs_tan * away + probs * away_tan)
    q_cot = scale * dot3(ss, ks, NN)
    q_cot_tan = scale * (dot3(dss, ks, NN) + dot3(ss, dks, NN))
    k_cot = dot3(ss, qs, TN)
    k_cot_tan = dot3(dss, qs, TN) + dot3(ss, dqs, TN)
    q_tan = normalize_back(qn, dqn, q_inverse, q_shift, q_cot, q_cot_tan)
    k_tan = normalize_back(kn, dkn, k_inverse, k_shift, k_cot, k_cot_tan)
    return mixed_tan, q_tan, k_tan, v_tan


def sums_kernel(rows, cots, rows_b, cots_b, w_rows, w_cots, w_rows_b, w_cots_b, out):
    front = dot(rows[...], w_rows[...], NN) + dot(rows_b[...], w_rows_b[...], NN)
    back = dot(cots[...], w_cots[...], NT) + dot(cots_b[...], w_cots_b[...], NT)
    hidden = (w_rows.shape[1] - 3 * HD) // 2
    high, low = halves(front[:, :HD])
    out[:, :HD] = high
    out[:, HD : 2 * HD] = low
    out[:, 2 * HD : 4 * HD] = front[:, HD : 3 * HD].astype(BF16)
    out[:, 4 * HD : 5 * HD] = back[:, :HD].astype(BF16)
    out[:, 5 * HD : 5 * HD + 2 * hidden] = front[:, 3 * HD :].astype(BF16)
    out[:, 5 * HD + 2 * hidden :] = back[:, HD:].astype(BF16)


def results_kernel(core, mine, theirs, rows, cots, qkv_out, out_out, up_out, down_out):
    first = core[0] == 0
    zero = jnp.where(first, mine[...], theirs[...])
    one = jnp.where(first, theirs[...], mine[...])

    def wide(x, at):
        return x[:, at * HD : (at + 1) * HD].astype(F32) + x[:, (at + 4) * HD : (at + 5) * HD].astype(F32)

    q, v, tq, cot = (wide(zero, at) for at in range(4))
    k, tk, tv, cot_tan = (wide(one, at) for at in range(4))
    mixed, q_tan, k_tan, v_tan = attention(q, k, v, tq, tk, tv, cot, cot_tan)
    rows_all, cots_all = rows[...], cots[...]
    hidden = (zero.shape[1] - 8 * HD) // 2
    for at, part in enumerate((zero, one)):
        place = slice(at * hidden, (at + 1) * hidden)
        act = part[:, 8 * HD : 8 * HD + hidden]
        hid = part[:, 8 * HD + hidden :]
        up_out[:, place] = dot(rows_all, hid, TN).astype(BF16)
        down_out[place, :] = dot(act, cots_all, TN).astype(BF16)
    for at, part in enumerate((q_tan, k_tan, v_tan)):
        qkv_out[at] = dot(rows_all, part.astype(BF16), TN).astype(BF16)
    out_out[...] = dot(mixed.astype(BF16), cots_all, TN).astype(BF16)


def hidden_pair(pre, cot_in):
    result, pull = jax.vjp(jax.nn.gelu, pre)
    return (result, pull(cot_in)[0])


def body(patches, cotangent, w_qkv, w_out, w_up, w_down, dir_qkv, dir_out, dir_up, dir_down):
    wide = lax.axis_size("mx")
    long = lax.axis_size("my")
    chips = wide // 2
    core = lax.rem(lax.axis_index("mx"), 2)
    ring = [[chip * 2 + c for chip in range(chips)] for c in range(2)]
    swap = [(i, i ^ 1) for i in range(wide)]
    width = w_qkv.shape[0]
    hidden = w_up.shape[1] // 2
    count = patches.shape[0] * long
    share = count // chips

    both = jnp.stack([patches, cotangent])
    gathered = lax.all_to_all(jnp.broadcast_to(both, (long,) + both.shape), "my", 0, 0, tiled=True)
    swapped = lax.ppermute(gathered, "mx", swap)

    def pick(at):
        zero = jnp.concatenate([w_qkv[:, 0], w_qkv[:, 2], dir_qkv[:, 0]], axis=1)
        one = jnp.concatenate([w_qkv[:, 1], dir_qkv[:, 1], dir_qkv[:, 2]], axis=1)
        cut = lambda a, dim: lax.dynamic_slice_in_dim(a, at * hidden, hidden, dim)
        front = [jnp.where(at == 0, zero, one), cut(w_up, 1), cut(dir_up, 1)]
        back = [jnp.where(at == 0, w_out, dir_out), cut(w_down, 0), cut(dir_down, 0)]
        return jnp.concatenate(front, axis=1), jnp.concatenate(back, axis=0)

    kept = pick(core)
    lent = pick(1 - core)
    taken = tuple(lax.ppermute(a, "mx", swap) for a in lent)

    flat = lambda a, at: a[:, at].reshape(count, width)
    rows, cots = flat(gathered, 0), flat(gathered, 1)
    columns = 5 * HD + 4 * hidden
    message = pl.pallas_call(
        sums_kernel,
        out_shape=jax.ShapeDtypeStruct((count, columns), BF16),
        in_specs=[VMEM] * 8,
        out_specs=VMEM,
        compiler_params=pltpu.CompilerParams(vmem_limit_bytes=48 * 2**20),
        name="sums",
    )(rows, cots, flat(swapped, 0), flat(swapped, 1), *kept, *taken)
    parts = lax.all_to_all(
        message.reshape(chips, share, columns), "mx", 0, 0, tiled=True, axis_index_groups=ring
    )
    sums = jnp.sum(parts.astype(F32), axis=0)
    attn = jnp.concatenate([sums[:, :HD] + sums[:, HD : 2 * HD], sums[:, 2 * HD : 5 * HD]], axis=1)
    pre_hidden, tan_hidden, cot_act, tan_act = jnp.split(sums[:, 5 * HD :], 4, axis=1)
    hid_tan = jax.jvp(hidden_pair, (pre_hidden, cot_act), (tan_hidden, tan_act))[1]
    attn_high = lax.reduce_precision(attn, 8, 7)
    reply = jnp.concatenate([attn_high, attn - attn_high, hid_tan[0], hid_tan[1]], axis=1).astype(BF16)
    mine = lax.all_to_all(
        jnp.broadcast_to(reply, (chips,) + reply.shape),
        "mx",
        0,
        0,
        tiled=True,
        axis_index_groups=ring,
    ).reshape(count, -1)
    theirs = lax.ppermute(mine, "mx", swap)
    hvp_qkv, hvp_out, hvp_up, hvp_down = pl.pallas_call(
        results_kernel,
        out_shape=(
            jax.ShapeDtypeStruct((3, width, HD), BF16),
            jax.ShapeDtypeStruct(w_out.shape, BF16),
            jax.ShapeDtypeStruct(w_up.shape, BF16),
            jax.ShapeDtypeStruct(w_down.shape, BF16),
        ),
        in_specs=[SMEM] + [VMEM] * 4,
        out_specs=(VMEM,) * 4,
        compiler_params=pltpu.CompilerParams(vmem_limit_bytes=48 * 2**20),
        name="results",
    )(core.reshape(1).astype(jnp.int32), mine, theirs, rows, cots)
    return jnp.transpose(hvp_qkv, (1, 0, 2)), hvp_out, hvp_up, hvp_down


def solution(mesh):
    return jax.shard_map(
        body,
        mesh=mesh,
        in_specs=(
            P("my", "mx"),
            P("my", "mx"),
            P("mx", None, "my"),
            P("my", "mx"),
            P("mx", "my"),
            P("my", "mx"),
            P("mx", None, "my"),
            P("my", "mx"),
            P("mx", "my"),
            P("my", "mx"),
        ),
        out_specs=(P("mx", None, "my"), P("my", "mx"), P("mx", "my"), P("my", "mx")),
        check_vma=False,
    )
```

```python
import math

import jax
import jax.numpy as jnp
from jax import lax
from jax.experimental import pallas as pl
from jax.experimental.pallas import tpu as pltpu
from jax.sharding import PartitionSpec as P

HD = 128
F32 = jnp.float32
BF16 = jnp.bfloat16
VMEM = pl.BlockSpec(memory_space=pltpu.VMEM)
SMEM = pl.BlockSpec(memory_space=pltpu.SMEM)

NN = ((1,), (0,))
NT = ((1,), (1,))
TN = ((0,), (0,))


def dot(left, right, dims):
    return lax.dot_general(left, right, (dims, ((), ())), preferred_element_type=F32)


def halves(x):
    high = x.astype(BF16)
    return high, (x - high.astype(F32)).astype(BF16)


def dot3(left, right, dims):
    return (
        dot(left[0], right[0], dims) + dot(left[0], right[1], dims) + dot(left[1], right[0], dims)
    )


def low_code(x, high):
    rest = (x - high) / jnp.where(high == 0.0, 1.0, high)
    return jnp.clip(jnp.floor(rest * 512.0 + 2.0), 0.0, 3.0)


def with_code(high, code):
    return high + high * ((code - 1.5) / 512.0)


def split_codes(packed):
    codes = []
    for place in (64.0, 16.0, 4.0):
        codes.insert(0, jnp.floor(packed / place))
        packed = packed - place * codes[0]
    return [packed] + codes


def mean(x):
    return jnp.mean(x, axis=-1, keepdims=True)


def total(x):
    return jnp.sum(x, axis=-1, keepdims=True)


def centre(x):
    return x - mean(x)


def normalize(x, x_tan):
    centred = centre(x)
    inverse = lax.rsqrt(mean(centred * centred) + 1e-06)
    y = centred * inverse
    shift = mean(y * x_tan)
    return y, (centre(x_tan) - y * shift) * inverse, inverse, shift


def normalize_back(y, y_tan, inverse, shift, cot, cot_tan):
    along = mean(y * cot)
    back = (centre(cot) - y * along) * inverse
    along_tan = mean(y_tan * cot) + mean(y * cot_tan)
    return (centre(cot_tan) - y_tan * along - y * along_tan - back * shift) * inverse


def attention(q, k, v, tq, tk, tv, cot, cot_tan):
    scale = 1.0 / math.sqrt(HD)
    qn, dqn, q_inverse, q_shift = normalize(q, tq)
    kn, dkn, k_inverse, k_shift = normalize(k, tk)
    qs, dqs, ks, dks = halves(qn * scale), halves(dqn * scale), halves(kn), halves(dkn)
    vs, dvs, cs, dcs = halves(v), halves(tv), halves(cot), halves(cot_tan)
    raised = jnp.exp(dot3(qs, ks, NT))
    probs = raised / total(raised)
    score_tan = dot3(dqs, ks, NT) + dot3(qs, dks, NT)
    probs_tan = probs * (score_tan - total(probs * score_tan))
    ps, dps = halves(probs), halves(probs_tan)
    mixed_tan = dot3(dps, vs, NN) + dot3(ps, dvs, NN)
    v_tan = dot3(dps, cs, TN) + dot3(ps, dcs, TN)
    cot_probs = dot3(cs, vs, NT)
    cot_probs_tan = dot3(dcs, vs, NT) + dot3(cs, dvs, NT)
    away = cot_probs - total(probs * cot_probs)
    away_tan = cot_probs_tan - total(probs_tan * cot_probs + probs * cot_probs_tan)
    ss, dss = halves(probs * away), halves(probs_tan * away + probs * away_tan)
    q_cot = scale * dot3(ss, ks, NN)
    q_cot_tan = scale * (dot3(dss, ks, NN) + dot3(ss, dks, NN))
    k_cot = dot3(ss, qs, TN)
    k_cot_tan = dot3(dss, qs, TN) + dot3(ss, dqs, TN)
    q_tan = normalize_back(qn, dqn, q_inverse, q_shift, q_cot, q_cot_tan)
    k_tan = normalize_back(kn, dkn, k_inverse, k_shift, k_cot, k_cot_tan)
    return mixed_tan, q_tan, k_tan, v_tan


def copies_kernel(patches, cotangent, out):
    both = jnp.concatenate([patches[...].astype(F32), cotangent[...].astype(F32)], axis=0)
    for at in range(out.shape[0]):
        out[at] = both.astype(BF16)


def sums_kernel(rows, cots, rows_b, cots_b, w_rows, w_cots, w_rows_b, w_cots_b, out):
    front = dot(rows[...], w_rows[...], NN) + dot(rows_b[...], w_rows_b[...], NN)
    back = dot(cots[...], w_cots[...], NT) + dot(cots_b[...], w_cots_b[...], NT)
    hidden = (w_rows.shape[1] - 3 * HD) // 2
    blocks = [front[:, at * HD : (at + 1) * HD] for at in range(3)] + [back[:, :HD]]
    packed = 0.0
    for at, block in enumerate(blocks):
        high = block.astype(BF16)
        out[:, at * HD : (at + 1) * HD] = high
        packed = packed + low_code(block, high.astype(F32)) * 4.0**at
    out[:, 4 * HD : 5 * HD] = packed.astype(BF16)
    out[:, 5 * HD : 5 * HD + 2 * hidden] = front[:, 3 * HD :].astype(BF16)
    out[:, 5 * HD + 2 * hidden :] = back[:, HD:].astype(BF16)


def results_kernel(
    core, mine, theirs, rows, cots, qkv_out, out_out, up_out, down_out, qkv, out, up, down, sems
):
    first = core[0] == 0
    zero = jnp.where(first, mine[...], theirs[...])
    one = jnp.where(first, theirs[...], mine[...])
    rows_all, cots_all = rows[...], cots[...]
    hidden = (zero.shape[1] - 5 * HD) // 2
    for at, part in enumerate((zero, one)):
        place = slice(at * hidden, (at + 1) * hidden)
        act = part[:, 5 * HD : 5 * HD + hidden]
        hid = part[:, 5 * HD + hidden :]
        up[:, place] = dot(rows_all, hid, TN).astype(BF16)
        down[place, :] = dot(act, cots_all, TN).astype(BF16)
    up_copy = pltpu.make_async_copy(up, up_out, sems.at[0])
    down_copy = pltpu.make_async_copy(down, down_out, sems.at[1])
    up_copy.start()
    down_copy.start()

    def blocks(part):
        codes = split_codes(part[:, 4 * HD : 5 * HD].astype(F32))
        highs = [part[:, at * HD : (at + 1) * HD].astype(F32) for at in range(4)]
        return [with_code(high, code) for high, code in zip(highs, codes)]

    q, v, tq, cot = blocks(zero)
    k, tk, tv, cot_tan = blocks(one)
    mixed, q_tan, k_tan, v_tan = attention(q, k, v, tq, tk, tv, cot, cot_tan)
    for at, part in enumerate((q_tan, k_tan, v_tan)):
        qkv[at] = dot(rows_all, part.astype(BF16), TN).astype(BF16)
    out[...] = dot(mixed.astype(BF16), cots_all, TN).astype(BF16)
    qkv_copy = pltpu.make_async_copy(qkv, qkv_out, sems.at[2])
    out_copy = pltpu.make_async_copy(out, out_out, sems.at[3])
    qkv_copy.start()
    out_copy.start()
    up_copy.wait()
    down_copy.wait()
    qkv_copy.wait()
    out_copy.wait()


def hidden_pair(pre, cot_in):
    result, pull = jax.vjp(jax.nn.gelu, pre)
    return (result, pull(cot_in)[0])


def body(patches, cotangent, w_qkv, w_out, w_up, w_down, dir_qkv, dir_out, dir_up, dir_down):
    wide = lax.axis_size("mx")
    long = lax.axis_size("my")
    chips = wide // 2
    core = lax.rem(lax.axis_index("mx"), 2)
    ring = [[chip * 2 + c for chip in range(chips)] for c in range(2)]
    swap = [(i, i ^ 1) for i in range(wide)]
    width = w_qkv.shape[0]
    hidden = w_up.shape[1] // 2
    count = patches.shape[0] * long
    share = count // chips

    own_rows = patches.shape[0]
    copies = pl.pallas_call(
        copies_kernel,
        out_shape=jax.ShapeDtypeStruct((long, 2 * own_rows, width), BF16),
        in_specs=[VMEM] * 2,
        out_specs=VMEM,
        name="copies",
    )(patches, cotangent)
    gathered = lax.all_to_all(copies, "my", 0, 0, tiled=True)
    swapped = lax.ppermute(gathered, "mx", swap)

    def pick(at):
        zero = jnp.concatenate([w_qkv[:, 0], w_qkv[:, 2], dir_qkv[:, 0]], axis=1)
        one = jnp.concatenate([w_qkv[:, 1], dir_qkv[:, 1], dir_qkv[:, 2]], axis=1)
        cut = lambda a, dim: lax.dynamic_slice_in_dim(a, at * hidden, hidden, dim)
        front = [jnp.where(at == 0, zero, one), cut(w_up, 1), cut(dir_up, 1)]
        back = [jnp.where(at == 0, w_out, dir_out), cut(w_down, 0), cut(dir_down, 0)]
        return jnp.concatenate(front, axis=1), jnp.concatenate(back, axis=0)

    kept = pick(core)
    lent = pick(1 - core)
    taken = tuple(lax.ppermute(a, "mx", swap) for a in lent)

    flat = lambda a, at: a[:, at * own_rows : (at + 1) * own_rows].reshape(count, width)
    rows, cots = flat(gathered, 0), flat(gathered, 1)
    columns = 5 * HD + 4 * hidden
    message = pl.pallas_call(
        sums_kernel,
        out_shape=jax.ShapeDtypeStruct((count, columns), BF16),
        in_specs=[VMEM] * 8,
        out_specs=VMEM,
        compiler_params=pltpu.CompilerParams(vmem_limit_bytes=48 * 2**20),
        name="sums",
    )(rows, cots, flat(swapped, 0), flat(swapped, 1), *kept, *taken)
    parts = lax.all_to_all(
        message.reshape(chips, share, columns), "mx", 0, 0, tiled=True, axis_index_groups=ring
    )
    wide_parts = parts.astype(F32)
    block = lambda a, at: a[..., at * HD : (at + 1) * HD]
    codes = split_codes(block(wide_parts, 4))
    sums = [jnp.sum(with_code(block(wide_parts, at), codes[at]), axis=0) for at in range(4)]
    highs = [lax.reduce_precision(a, 8, 7) for a in sums]
    packed = sum(low_code(a, high) * 4.0**at for at, (a, high) in enumerate(zip(sums, highs)))
    hidden_sums = jnp.sum(wide_parts[..., 5 * HD :], axis=0)
    pre_hidden, tan_hidden, cot_act, tan_act = jnp.split(hidden_sums, 4, axis=1)
    hid_tan = jax.jvp(hidden_pair, (pre_hidden, cot_act), (tan_hidden, tan_act))[1]
    reply = jnp.concatenate(highs + [packed, hid_tan[0], hid_tan[1]], axis=1).astype(BF16)
    mine = lax.all_to_all(
        jnp.broadcast_to(reply, (chips,) + reply.shape),
        "mx",
        0,
        0,
        tiled=True,
        axis_index_groups=ring,
    ).reshape(count, -1)
    theirs = lax.ppermute(mine, "mx", swap)
    shapes = ((3, width, HD), w_out.shape, w_up.shape, w_down.shape)
    hvp_qkv, hvp_out, hvp_up, hvp_down = pl.pallas_call(
        results_kernel,
        out_shape=tuple(jax.ShapeDtypeStruct(shape, BF16) for shape in shapes),
        in_specs=[SMEM] + [VMEM] * 4,
        out_specs=(pl.BlockSpec(memory_space=pl.ANY),) * 4,
        scratch_shapes=[pltpu.VMEM(shape, BF16) for shape in shapes]
        + [pltpu.SemaphoreType.DMA((4,))],
        compiler_params=pltpu.CompilerParams(vmem_limit_bytes=48 * 2**20),
        name="results",
    )(core.reshape(1).astype(jnp.int32), mine, theirs, rows, cots)
    return jnp.transpose(hvp_qkv, (1, 0, 2)), hvp_out, hvp_up, hvp_down


def solution(mesh):
    return jax.shard_map(
        body,
        mesh=mesh,
        in_specs=(
            P("my", "mx"),
            P("my", "mx"),
            P("mx", None, "my"),
            P("my", "mx"),
            P("mx", "my"),
            P("my", "mx"),
            P("mx", None, "my"),
            P("my", "mx"),
            P("mx", "my"),
            P("my", "mx"),
        ),
        out_specs=(P("mx", None, "my"), P("my", "mx"), P("mx", "my"), P("my", "mx")),
        check_vma=False,
    )
```

```python
import math

import jax
import jax.numpy as jnp
from jax import lax
from jax.experimental import pallas as pl
from jax.experimental.pallas import tpu as pltpu
from jax.sharding import PartitionSpec as P

HD = 128
F32 = jnp.float32
BF16 = jnp.bfloat16
VMEM = pl.BlockSpec(memory_space=pltpu.VMEM)
SMEM = pl.BlockSpec(memory_space=pltpu.SMEM)

NN = ((1,), (0,))
NT = ((1,), (1,))
TN = ((0,), (0,))


def dot(left, right, dims):
    return lax.dot_general(left, right, (dims, ((), ())), preferred_element_type=F32)


def halves(x):
    high = x.astype(BF16)
    return high, (x - high.astype(F32)).astype(BF16)


def product(pairs, dims):
    left = [part for (high, low), _ in pairs for part in (high, high, low)]
    right = [part for _, (high, low) in pairs for part in (high, low, high)]
    return dot(
        jnp.concatenate(left, axis=dims[0][0]), jnp.concatenate(right, axis=dims[1][0]), dims
    )


def low_code(x, high):
    rest = (x - high) / jnp.where(high == 0.0, 1.0, high)
    return jnp.clip(jnp.floor(rest * 512.0 + 2.0), 0.0, 3.0)


def with_code(high, code):
    return high + high * ((code - 1.5) / 512.0)


def split_codes(packed):
    codes = []
    for place in (64.0, 16.0, 4.0):
        codes.insert(0, jnp.floor(packed / place))
        packed = packed - place * codes[0]
    return [packed] + codes


def mean(x):
    return jnp.mean(x, axis=-1, keepdims=True)


def total(x):
    return jnp.sum(x, axis=-1, keepdims=True)


def centre(x):
    return x - mean(x)


def normalize(x, x_tan):
    centred = centre(x)
    inverse = lax.rsqrt(mean(centred * centred) + 1e-06)
    y = centred * inverse
    shift = mean(y * x_tan)
    return y, (centre(x_tan) - y * shift) * inverse, inverse, shift


def normalize_back(y, y_tan, inverse, shift, cot, cot_tan):
    along = mean(y * cot)
    back = (centre(cot) - y * along) * inverse
    along_tan = mean(y_tan * cot) + mean(y * cot_tan)
    return (centre(cot_tan) - y_tan * along - y * along_tan - back * shift) * inverse


def attention(q, k, v, tq, tk, tv, cot, cot_tan):
    scale = 1.0 / math.sqrt(HD)
    qn, dqn, q_inverse, q_shift = normalize(q, tq)
    kn, dkn, k_inverse, k_shift = normalize(k, tk)
    qs, dqs, ks, dks = halves(qn * scale), halves(dqn * scale), halves(kn), halves(dkn)
    vs, dvs, cs, dcs = halves(v), halves(tv), halves(cot), halves(cot_tan)
    raised = jnp.exp(product([(qs, ks)], NT))
    probs = raised / total(raised)
    score_tan = product([(dqs, ks), (qs, dks)], NT)
    probs_tan = probs * (score_tan - total(probs * score_tan))
    ps, dps = halves(probs), halves(probs_tan)
    mixed_tan = product([(dps, vs), (ps, dvs)], NN)
    v_tan = product([(dps, cs), (ps, dcs)], TN)
    cot_probs = product([(cs, vs)], NT)
    cot_probs_tan = product([(dcs, vs), (cs, dvs)], NT)
    away = cot_probs - total(probs * cot_probs)
    away_tan = cot_probs_tan - total(probs_tan * cot_probs + probs * cot_probs_tan)
    ss, dss = halves(probs * away), halves(probs_tan * away + probs * away_tan)
    q_cot = scale * product([(ss, ks)], NN)
    q_cot_tan = scale * product([(dss, ks), (ss, dks)], NN)
    k_cot = product([(ss, qs)], TN)
    k_cot_tan = product([(dss, qs), (ss, dqs)], TN)
    q_tan = normalize_back(qn, dqn, q_inverse, q_shift, q_cot, q_cot_tan)
    k_tan = normalize_back(kn, dkn, k_inverse, k_shift, k_cot, k_cot_tan)
    return mixed_tan, q_tan, k_tan, v_tan


def own_sums_kernel(rows, cots, w_rows, w_cots, front, back):
    front[...] = dot(rows[...], w_rows[...], NN)
    back[...] = dot(cots[...], w_cots[...], NT)


def sums_kernel(front_a, back_a, rows, cots, w_rows, w_cots, out):
    front = front_a[...] + dot(rows[...], w_rows[...], NN)
    back = back_a[...] + dot(cots[...], w_cots[...], NT)
    hidden = (w_rows.shape[1] - 3 * HD) // 2
    blocks = [front[:, at * HD : (at + 1) * HD] for at in range(3)] + [back[:, :HD]]
    packed = 0.0
    for at, block in enumerate(blocks):
        high = block.astype(BF16)
        out[:, at * HD : (at + 1) * HD] = high
        packed = packed + low_code(block, high.astype(F32)) * 4.0**at
    out[:, 4 * HD : 5 * HD] = packed.astype(BF16)
    out[:, 5 * HD : 5 * HD + 2 * hidden] = front[:, 3 * HD :].astype(BF16)
    out[:, 5 * HD + 2 * hidden :] = back[:, HD:].astype(BF16)


def hidden_products(part, rows, cots):
    hidden = (part.shape[1] - 5 * HD) // 2
    act = part[:, 5 * HD : 5 * HD + hidden]
    hid = part[:, 5 * HD + hidden :]
    return dot(rows, hid, TN).astype(BF16), dot(act, cots, TN).astype(BF16)


def own_products_kernel(mine, rows, cots, up, down):
    up[...], down[...] = hidden_products(mine[...], rows[...], cots[...])


def results_kernel(
    core, mine, theirs, rows, cots, own_up, own_down,
    qkv_out, out_out, up_out, down_out,
    qkv, out, up, down, sems,
):
    first = core[0] == 0
    rows_all, cots_all = rows[...], cots[...]
    other_up, other_down = hidden_products(theirs[...], rows_all, cots_all)
    hidden = other_down.shape[0]
    up[:, :hidden] = jnp.where(first, own_up[...], other_up)
    up[:, hidden:] = jnp.where(first, other_up, own_up[...])
    down[:hidden, :] = jnp.where(first, own_down[...], other_down)
    down[hidden:, :] = jnp.where(first, other_down, own_down[...])
    up_copy = pltpu.make_async_copy(up, up_out, sems.at[0])
    down_copy = pltpu.make_async_copy(down, down_out, sems.at[1])
    up_copy.start()
    down_copy.start()
    zero = jnp.where(first, mine[:, : 5 * HD], theirs[:, : 5 * HD])
    one = jnp.where(first, theirs[:, : 5 * HD], mine[:, : 5 * HD])

    def blocks(part):
        codes = split_codes(part[:, 4 * HD : 5 * HD].astype(F32))
        highs = [part[:, at * HD : (at + 1) * HD].astype(F32) for at in range(4)]
        return [with_code(high, code) for high, code in zip(highs, codes)]

    q, v, tq, cot = blocks(zero)
    k, tk, tv, cot_tan = blocks(one)
    mixed, q_tan, k_tan, v_tan = attention(q, k, v, tq, tk, tv, cot, cot_tan)
    for at, part in enumerate((q_tan, k_tan, v_tan)):
        qkv[at] = dot(rows_all, part.astype(BF16), TN).astype(BF16)
    out[...] = dot(mixed.astype(BF16), cots_all, TN).astype(BF16)
    qkv_copy = pltpu.make_async_copy(qkv, qkv_out, sems.at[2])
    out_copy = pltpu.make_async_copy(out, out_out, sems.at[3])
    qkv_copy.start()
    out_copy.start()
    up_copy.wait()
    down_copy.wait()
    qkv_copy.wait()
    out_copy.wait()


def hidden_pair(pre, cot_in):
    result, pull = jax.vjp(jax.nn.gelu, pre)
    return (result, pull(cot_in)[0])


def body(patches, cotangent, w_qkv, w_out, w_up, w_down, dir_qkv, dir_out, dir_up, dir_down):
    wide = lax.axis_size("mx")
    long = lax.axis_size("my")
    chips = wide // 2
    core = lax.rem(lax.axis_index("mx"), 2)
    ring = [[chip * 2 + c for chip in range(chips)] for c in range(2)]
    swap = [(i, i ^ 1) for i in range(wide)]
    width = w_qkv.shape[0]
    hidden = w_up.shape[1] // 2
    count = patches.shape[0] * long
    share = count // chips

    own_rows = patches.shape[0]
    copy_shape = (long, 2, own_rows, width)
    copies = jnp.where(
        lax.broadcasted_iota(jnp.int32, copy_shape, 1) == 0,
        jnp.broadcast_to(patches, copy_shape),
        jnp.broadcast_to(cotangent, copy_shape),
    )
    gathered = lax.all_to_all(copies, "my", 0, 0, tiled=True)
    swapped = lax.ppermute(gathered, "mx", swap)

    def pick(at):
        zero = jnp.concatenate([w_qkv[:, 0], w_qkv[:, 2], dir_qkv[:, 0]], axis=1)
        one = jnp.concatenate([w_qkv[:, 1], dir_qkv[:, 1], dir_qkv[:, 2]], axis=1)
        cut = lambda a, dim: lax.dynamic_slice_in_dim(a, at * hidden, hidden, dim)
        front = [jnp.where(at == 0, zero, one), cut(w_up, 1), cut(dir_up, 1)]
        back = [jnp.where(at == 0, w_out, dir_out), cut(w_down, 0), cut(dir_down, 0)]
        return jnp.concatenate(front, axis=1), jnp.concatenate(back, axis=0)

    kept = pick(core)
    lent = pick(1 - core)
    taken = tuple(lax.ppermute(a, "mx", swap) for a in lent)

    flat = lambda a, at: a[:, at].reshape(count, width)
    rows, cots = flat(gathered, 0), flat(gathered, 1)
    columns = 5 * HD + 4 * hidden
    widths = (3 * HD + 2 * hidden, HD + 2 * hidden)
    room = pltpu.CompilerParams(vmem_limit_bytes=48 * 2**20)
    sums_cost = pl.CostEstimate(
        flops=2 * count * width * sum(widths),
        bytes_accessed=2 * width * sum(widths) + 4 * count * sum(widths),
        transcendentals=0,
    )
    own_sums = pl.pallas_call(
        own_sums_kernel,
        out_shape=tuple(jax.ShapeDtypeStruct((count, n), F32) for n in widths),
        in_specs=[VMEM] * 4,
        out_specs=(VMEM,) * 2,
        compiler_params=room,
        cost_estimate=sums_cost,
        name="own_sums",
    )(rows, cots, *kept)
    message = pl.pallas_call(
        sums_kernel,
        out_shape=jax.ShapeDtypeStruct((count, columns), BF16),
        in_specs=[VMEM] * 6,
        out_specs=VMEM,
        compiler_params=room,
        cost_estimate=sums_cost,
        name="sums",
    )(*own_sums, flat(swapped, 0), flat(swapped, 1), *taken)
    parts = lax.all_to_all(
        message.reshape(chips, share, columns), "mx", 0, 0, tiled=True, axis_index_groups=ring
    )
    wide_parts = parts.astype(F32)
    block = lambda a, at: a[..., at * HD : (at + 1) * HD]
    codes = split_codes(block(wide_parts, 4))
    sums = [jnp.sum(with_code(block(wide_parts, at), codes[at]), axis=0) for at in range(4)]
    highs = [lax.reduce_precision(a, 8, 7) for a in sums]
    packed = sum(low_code(a, high) * 4.0**at for at, (a, high) in enumerate(zip(sums, highs)))
    hidden_sums = jnp.sum(wide_parts[..., 5 * HD :], axis=0)
    pre_hidden, tan_hidden, cot_act, tan_act = jnp.split(hidden_sums, 4, axis=1)
    hid_tan = jax.jvp(hidden_pair, (pre_hidden, cot_act), (tan_hidden, tan_act))[1]
    reply = jnp.concatenate(highs + [packed, hid_tan[0], hid_tan[1]], axis=1).astype(BF16)
    mine = lax.all_to_all(
        jnp.broadcast_to(reply, (chips,) + reply.shape),
        "mx",
        0,
        0,
        tiled=True,
        axis_index_groups=ring,
    ).reshape(count, -1)
    theirs = lax.ppermute(mine, "mx", swap)
    own_products = pl.pallas_call(
        own_products_kernel,
        out_shape=(
            jax.ShapeDtypeStruct((width, hidden), BF16),
            jax.ShapeDtypeStruct((hidden, width), BF16),
        ),
        in_specs=[VMEM] * 3,
        out_specs=(VMEM,) * 2,
        compiler_params=room,
        cost_estimate=pl.CostEstimate(
            flops=4 * count * width * hidden,
            bytes_accessed=4 * width * hidden + 8 * count * width,
            transcendentals=0,
        ),
        name="own_products",
    )(mine, rows, cots)
    shapes = ((3, width, HD), w_out.shape, w_up.shape, w_down.shape)
    hvp_qkv, hvp_out, hvp_up, hvp_down = pl.pallas_call(
        results_kernel,
        out_shape=tuple(jax.ShapeDtypeStruct(shape, BF16) for shape in shapes),
        in_specs=[SMEM] + [VMEM] * 6,
        out_specs=(pl.BlockSpec(memory_space=pl.ANY),) * 4,
        scratch_shapes=[pltpu.VMEM(shape, BF16) for shape in shapes]
        + [pltpu.SemaphoreType.DMA((4,))],
        compiler_params=room,
        name="results",
    )(core.reshape(1).astype(jnp.int32), mine, theirs, rows, cots, *own_products)
    return jnp.transpose(hvp_qkv, (1, 0, 2)), hvp_out, hvp_up, hvp_down


def solution(mesh):
    return jax.shard_map(
        body,
        mesh=mesh,
        in_specs=(
            P("my", "mx"),
            P("my", "mx"),
            P("mx", None, "my"),
            P("my", "mx"),
            P("mx", "my"),
            P("my", "mx"),
            P("mx", None, "my"),
            P("my", "mx"),
            P("mx", "my"),
            P("my", "mx"),
        ),
        out_specs=(P("mx", None, "my"), P("my", "mx"), P("mx", "my"), P("my", "mx")),
        check_vma=False,
    )
```

```python
import math

import jax
import jax.numpy as jnp
from jax import lax
from jax.experimental import pallas as pl
from jax.experimental.pallas import tpu as pltpu
from jax.sharding import PartitionSpec as P

HD = 128
F32 = jnp.float32
BF16 = jnp.bfloat16
VMEM = pl.BlockSpec(memory_space=pltpu.VMEM)
SMEM = pl.BlockSpec(memory_space=pltpu.SMEM)

NN = ((1,), (0,))
NT = ((1,), (1,))
TN = ((0,), (0,))


def dot(left, right, dims):
    return lax.dot_general(left, right, (dims, ((), ())), preferred_element_type=F32)


def halves(x):
    high = x.astype(BF16)
    return high, (x - high.astype(F32)).astype(BF16)


def product(pairs, dims):
    left = [part for (high, low), _ in pairs for part in (high, high, low)]
    right = [part for _, (high, low) in pairs for part in (high, low, high)]
    return dot(
        jnp.concatenate(left, axis=dims[0][0]), jnp.concatenate(right, axis=dims[1][0]), dims
    )


def low_code(x, high):
    rest = (x - high) / jnp.where(high == 0.0, 1.0, high)
    return jnp.clip(jnp.floor(rest * 512.0 + 2.0), 0.0, 3.0)


def with_code(high, code):
    return high + high * ((code - 1.5) / 512.0)


def split_codes(packed):
    codes = []
    for place in (64.0, 16.0, 4.0):
        codes.insert(0, jnp.floor(packed / place))
        packed = packed - place * codes[0]
    return [packed] + codes


def mean(x):
    return jnp.mean(x, axis=-1, keepdims=True)


def total(x):
    return jnp.sum(x, axis=-1, keepdims=True)


def centre(x):
    return x - mean(x)


def normalize(x, x_tan):
    centred = centre(x)
    inverse = lax.rsqrt(mean(centred * centred) + 1e-06)
    y = centred * inverse
    shift = mean(y * x_tan)
    return y, (centre(x_tan) - y * shift) * inverse, inverse, shift


def normalize_back(y, y_tan, inverse, shift, cot, cot_tan):
    along = mean(y * cot)
    back = (centre(cot) - y * along) * inverse
    along_tan = mean(y_tan * cot) + mean(y * cot_tan)
    return (centre(cot_tan) - y_tan * along - y * along_tan - back * shift) * inverse


def attention(q, k, v, tq, tk, tv, cot, cot_tan):
    scale = 1.0 / math.sqrt(HD)
    qn, dqn, q_inverse, q_shift = normalize(q, tq)
    kn, dkn, k_inverse, k_shift = normalize(k, tk)
    qs, dqs, ks, dks = halves(qn * scale), halves(dqn * scale), halves(kn), halves(dkn)
    vs, dvs, cs, dcs = halves(v), halves(tv), halves(cot), halves(cot_tan)
    raised = jnp.exp(product([(qs, ks)], NT))
    probs = raised / total(raised)
    score_tan = product([(dqs, ks), (qs, dks)], NT)
    probs_tan = probs * (score_tan - total(probs * score_tan))
    ps, dps = halves(probs), halves(probs_tan)
    mixed_tan = product([(dps, vs), (ps, dvs)], NN)
    v_tan = product([(dps, cs), (ps, dcs)], TN)
    cot_probs = product([(cs, vs)], NT)
    cot_probs_tan = product([(dcs, vs), (cs, dvs)], NT)
    away = cot_probs - total(probs * cot_probs)
    away_tan = cot_probs_tan - total(probs_tan * cot_probs + probs * cot_probs_tan)
    ss, dss = halves(probs * away), halves(probs_tan * away + probs * away_tan)
    q_cot = scale * product([(ss, ks)], NN)
    q_cot_tan = scale * product([(dss, ks), (ss, dks)], NN)
    k_cot = product([(ss, qs)], TN)
    k_cot_tan = product([(dss, qs), (ss, dqs)], TN)
    q_tan = normalize_back(qn, dqn, q_inverse, q_shift, q_cot, q_cot_tan)
    k_tan = normalize_back(kn, dkn, k_inverse, k_shift, k_cot, k_cot_tan)
    return mixed_tan, q_tan, k_tan, v_tan


def own_sums_kernel(rows, cots, w_rows, w_cots, front, back):
    front[...] = dot(rows[...], w_rows[...], NN)
    back[...] = dot(cots[...], w_cots[...], NT)


def attention_sums_kernel(front_a, back_a, rows, cots, w_rows, w_cots, out):
    front = front_a[:, : 6 * HD] + dot(rows[...], w_rows[:, : 6 * HD], NN)
    back = back_a[:, : 2 * HD] + dot(cots[...], w_cots[: 2 * HD, :], NT)
    packed = [0.0, 0.0]
    for at in range(8):
        block = front[:, at * HD : (at + 1) * HD] if at < 6 else back[:, (at - 6) * HD : (at - 5) * HD]
        high = block.astype(BF16)
        out[:, at * HD : (at + 1) * HD] = high
        packed[at // 4] += low_code(block, high.astype(F32)) * 4.0 ** (at % 4)
    out[:, 8 * HD : 9 * HD] = packed[0].astype(BF16)
    out[:, 9 * HD :] = packed[1].astype(BF16)


def hidden_sums_kernel(front_a, back_a, rows, cots, w_rows, w_cots, out):
    columns = w_rows.shape[1]
    out[:, :columns] = (front_a[...] + dot(rows[...], w_rows[...], NN)).astype(BF16)
    out[:, columns:] = (back_a[...] + dot(cots[...], w_cots[...], NT)).astype(BF16)


def attention_kernel(whole, out):
    blocks = []
    for group in range(2):
        codes = split_codes(whole[:, (8 + group) * HD : (9 + group) * HD].astype(F32))
        for at in range(4):
            place = 4 * group + at
            blocks.append(with_code(whole[:, place * HD : (place + 1) * HD].astype(F32), codes[at]))
    mixed, q_tan, k_tan, v_tan = attention(*blocks)
    for at, part in enumerate((q_tan, k_tan, v_tan, mixed)):
        out[:, at * HD : (at + 1) * HD] = part.astype(BF16)
    out[:, 4 * HD :] = jnp.zeros((out.shape[0], out.shape[1] - 4 * HD), BF16)


def products_kernel(role, lows, rows, cots, *refs):
    qkv_out, out_out, up_out, down_out, qkv, out, up, down, sems = refs[-9:]

    def write(pairs):
        copies = [pltpu.make_async_copy(*pair, sems.at[at]) for at, pair in enumerate(pairs)]
        for copy in copies:
            copy.start()
        for copy in copies:
            copy.wait()

    @pl.when(role[0] == 0)
    def _():
        for at in range(3):
            qkv[at] = dot(rows[...], lows[:, at * HD : (at + 1) * HD], TN).astype(BF16)
        out[...] = dot(lows[:, 3 * HD : 4 * HD], cots[...], TN).astype(BF16)
        write([(qkv, qkv_out), (out, out_out)])

    @pl.when(role[0] == 1)
    def _():
        hidden = down.shape[0]
        up[...] = dot(rows[...], lows[:, hidden:], TN).astype(BF16)
        down[...] = dot(lows[:, :hidden], cots[...], TN).astype(BF16)
        write([(up, up_out), (down, down_out)])


def hidden_pair(pre, cot_in):
    result, pull = jax.vjp(jax.nn.gelu, pre)
    return (result, pull(cot_in)[0])


def body(patches, cotangent, w_qkv, w_out, w_up, w_down, dir_qkv, dir_out, dir_up, dir_down):
    wide = lax.axis_size("mx")
    long = lax.axis_size("my")
    chips = wide // 2
    core = lax.rem(lax.axis_index("mx"), 2)
    ring = [[chip * 2 + c for chip in range(chips)] for c in range(2)]
    swap = [(i, i ^ 1) for i in range(wide)]
    width = w_qkv.shape[0]
    hidden = w_up.shape[1]
    count = patches.shape[0] * long
    share = count // chips

    own_rows = patches.shape[0]
    copy_shape = (long, 2, own_rows, width)
    copies = jnp.where(
        lax.broadcasted_iota(jnp.int32, copy_shape, 1) == 0,
        jnp.broadcast_to(patches, copy_shape),
        jnp.broadcast_to(cotangent, copy_shape),
    )
    gathered = lax.all_to_all(copies, "my", 0, 0, tiled=True)
    swapped = lax.ppermute(gathered, "mx", swap)

    first = core == 0
    flat = lambda a: [a[:, at] for at in range(3)]
    attn_front = jnp.concatenate(flat(w_qkv) + flat(dir_qkv), axis=1)
    attn_front = jnp.pad(attn_front, ((0, 0), (0, 2 * hidden - 6 * HD)))
    attn_back = jnp.pad(jnp.concatenate([w_out, dir_out]), ((0, 2 * hidden - 2 * HD), (0, 0)))
    hid_front = jnp.concatenate([w_up, dir_up], axis=1)
    hid_back = jnp.concatenate([w_down, dir_down])
    kept = (jnp.where(first, attn_front, hid_front), jnp.where(first, attn_back, hid_back))
    lent = (jnp.where(first, hid_front, attn_front), jnp.where(first, hid_back, attn_back))
    taken = tuple(lax.ppermute(a, "mx", swap) for a in lent)

    pick = lambda a, at: a[:, at].reshape(count, width)
    rows, cots = pick(gathered, 0), pick(gathered, 1)
    room = pltpu.CompilerParams(vmem_limit_bytes=48 * 2**20)
    own_sums = pl.pallas_call(
        own_sums_kernel,
        out_shape=(jax.ShapeDtypeStruct((count, 2 * hidden), F32),) * 2,
        in_specs=[VMEM] * 4,
        out_specs=(VMEM,) * 2,
        compiler_params=room,
        cost_estimate=pl.CostEstimate(
            flops=8 * count * width * hidden,
            bytes_accessed=8 * width * hidden + 16 * count * hidden,
            transcendentals=0,
        ),
        name="own_sums",
    )(rows, cots, *kept)

    def sums(kernel, columns, name, operands):
        message = pl.pallas_call(
            kernel,
            out_shape=jax.ShapeDtypeStruct((count, columns), BF16),
            in_specs=[VMEM] * 6,
            out_specs=VMEM,
            compiler_params=room,
            name=name,
        )(*operands)
        message = message.reshape(chips, share, columns)
        return lax.all_to_all(message, "mx", 0, 0, tiled=True, axis_index_groups=ring).astype(F32)

    def spread(reply):
        copies = jnp.broadcast_to(reply.astype(BF16), (chips,) + reply.shape)
        whole = lax.all_to_all(copies, "mx", 0, 0, tiled=True, axis_index_groups=ring)
        return whole.reshape(count, -1)

    def attention_part(*operands):
        parts = sums(attention_sums_kernel, 10 * HD, "attention_sums", operands)
        block = lambda at: parts[..., at * HD : (at + 1) * HD]
        reply, packed = [], []
        for group in range(2):
            codes = split_codes(block(8 + group))
            whole = [jnp.sum(with_code(block(4 * group + at), codes[at]), axis=0) for at in range(4)]
            highs = [lax.reduce_precision(a, 8, 7) for a in whole]
            reply += highs
            packed.append(sum(low_code(a, high) * 4.0**at for at, (a, high) in enumerate(zip(whole, highs))))
        return pl.pallas_call(
            attention_kernel,
            out_shape=jax.ShapeDtypeStruct((count, 2 * hidden), BF16),
            in_specs=[VMEM],
            out_specs=VMEM,
            compiler_params=room,
            name="attention",
        )(spread(jnp.concatenate(reply + packed, axis=1)))

    def hidden_part(*operands):
        parts = sums(hidden_sums_kernel, 4 * hidden, "hidden_sums", operands)
        whole = jnp.sum(parts, axis=0)
        pre_hidden, tan_hidden, cot_act, tan_act = jnp.split(whole, 4, axis=1)
        hid_tan = jax.jvp(hidden_pair, (pre_hidden, cot_act), (tan_hidden, tan_act))[1]
        return spread(jnp.concatenate(hid_tan, axis=1))

    lows = lax.cond(
        first,
        attention_part,
        hidden_part,
        *own_sums,
        pick(swapped, 0),
        pick(swapped, 1),
        *taken,
    )
    theirs = lax.ppermute(lows, "mx", swap)

    shapes = ((3, width, HD), w_out.shape, w_up.shape, w_down.shape)
    anywhere = pl.BlockSpec(memory_space=pl.ANY)

    def products(role, part, written, name):
        return pl.pallas_call(
            products_kernel,
            out_shape=tuple(jax.ShapeDtypeStruct(shape, BF16) for shape in shapes),
            in_specs=[SMEM] + [VMEM] * 3 + [anywhere] * len(written),
            out_specs=(anywhere,) * 4,
            scratch_shapes=[pltpu.VMEM(shape, BF16) for shape in shapes]
            + [pltpu.SemaphoreType.DMA((2,))],
            input_output_aliases={4 + at: at for at in range(len(written))},
            compiler_params=room,
            cost_estimate=pl.CostEstimate(
                flops=8 * count * width * hidden,
                bytes_accessed=8 * width * hidden,
                transcendentals=0,
            ),
            name=name,
        )(role.reshape(1).astype(jnp.int32), part, rows, cots, *written)

    written = products(core, lows, (), "own_products")
    hvp_qkv, hvp_out, hvp_up, hvp_down = products(1 - core, theirs, written, "other_products")
    return jnp.transpose(hvp_qkv, (1, 0, 2)), hvp_out, hvp_up, hvp_down


def solution(mesh):
    return jax.shard_map(
        body,
        mesh=mesh,
        in_specs=(
            P("my", "mx"),
            P("my", "mx"),
            P("mx", None, "my"),
            P("my", "mx"),
            P("mx", "my"),
            P("my", "mx"),
            P("mx", None, "my"),
            P("my", "mx"),
            P("mx", "my"),
            P("my", "mx"),
        ),
        out_specs=(P("mx", None, "my"), P("my", "mx"), P("mx", "my"), P("my", "mx")),
        check_vma=False,
    )
```

```python
import math

import jax
import jax.numpy as jnp
from jax import lax
from jax.experimental import pallas as pl
from jax.experimental.pallas import tpu as pltpu
from jax.sharding import PartitionSpec as P

HD = 128
F32 = jnp.float32
BF16 = jnp.bfloat16
VMEM = pl.BlockSpec(memory_space=pltpu.VMEM)
SMEM = pl.BlockSpec(memory_space=pltpu.SMEM)

NN = ((1,), (0,))
NT = ((1,), (1,))
TN = ((0,), (0,))


def dot(left, right, dims):
    return lax.dot_general(left, right, (dims, ((), ())), preferred_element_type=F32)


def halves(x):
    high = x.astype(BF16)
    return high, (x - high.astype(F32)).astype(BF16)


def product(pairs, dims):
    left = [part for (high, low), _ in pairs for part in (high, high, low)]
    right = [part for _, (high, low) in pairs for part in (high, low, high)]
    return dot(
        jnp.concatenate(left, axis=dims[0][0]), jnp.concatenate(right, axis=dims[1][0]), dims
    )


def low_code(x, high, levels):
    rest = (x - high) / jnp.where(high == 0.0, 1.0, high)
    return jnp.clip(jnp.floor((rest * 256.0 + 1.0) * (levels / 2)), 0.0, levels - 1.0)


def with_code(high, code, levels):
    return high + high * (((code + 0.5) * (2 / levels) - 1.0) / 256.0)


def split_codes(packed, levels, number):
    codes = []
    for place in range(number - 1, 0, -1):
        codes.insert(0, jnp.floor(packed / float(levels) ** place))
        packed = packed - float(levels) ** place * codes[0]
    return [packed] + codes


def mean(x):
    return jnp.mean(x, axis=-1, keepdims=True)


def total(x):
    return jnp.sum(x, axis=-1, keepdims=True)


def centre(x):
    return x - mean(x)


def normalize(x, x_tan):
    centred = centre(x)
    inverse = lax.rsqrt(mean(centred * centred) + 1e-06)
    y = centred * inverse
    shift = mean(y * x_tan)
    return y, (centre(x_tan) - y * shift) * inverse, inverse, shift


def normalize_back(y, y_tan, inverse, shift, cot, cot_tan):
    along = mean(y * cot)
    back = (centre(cot) - y * along) * inverse
    along_tan = mean(y_tan * cot) + mean(y * cot_tan)
    return (centre(cot_tan) - y_tan * along - y * along_tan - back * shift) * inverse


def attention(q, k, v, tq, tk, tv, cot, cot_tan):
    scale = 1.0 / math.sqrt(HD)
    qn, dqn, q_inverse, q_shift = normalize(q, tq)
    kn, dkn, k_inverse, k_shift = normalize(k, tk)
    qs, dqs, ks, dks = halves(qn * scale), halves(dqn * scale), halves(kn), halves(dkn)
    vs, dvs, cs, dcs = halves(v), halves(tv), halves(cot), halves(cot_tan)
    raised = jnp.exp(product([(qs, ks)], NT))
    probs = raised / total(raised)
    score_tan = product([(dqs, ks), (qs, dks)], NT)
    probs_tan = probs * (score_tan - total(probs * score_tan))
    ps, dps = halves(probs), halves(probs_tan)
    mixed_tan = product([(dps, vs), (ps, dvs)], NN)
    v_tan = product([(dps, cs), (ps, dcs)], TN)
    cot_probs = product([(cs, vs)], NT)
    cot_probs_tan = product([(dcs, vs), (cs, dvs)], NT)
    away = cot_probs - total(probs * cot_probs)
    away_tan = cot_probs_tan - total(probs_tan * cot_probs + probs * cot_probs_tan)
    ss, dss = halves(probs * away), halves(probs_tan * away + probs * away_tan)
    q_cot = scale * product([(ss, ks)], NN)
    q_cot_tan = scale * product([(dss, ks), (ss, dks)], NN)
    k_cot = product([(ss, qs)], TN)
    k_cot_tan = product([(dss, qs), (ss, dqs)], TN)
    q_tan = normalize_back(qn, dqn, q_inverse, q_shift, q_cot, q_cot_tan)
    k_tan = normalize_back(kn, dkn, k_inverse, k_shift, k_cot, k_cot_tan)
    return mixed_tan, q_tan, k_tan, v_tan


def own_sums_kernel(rows, cots, w_rows, w_cots, front, back):
    front[...] = dot(rows[...], w_rows[...], NN)
    back[...] = dot(cots[...], w_cots[...], NT)


def sums_kernel(role, front_a, back_a, rows, cots, w_rows, w_cots, out):
    @pl.when(role[0] == 0)
    def _():
        front = front_a[:, : 6 * HD] + dot(rows[...], w_rows[:, : 6 * HD], NN)
        back = back_a[:, : 2 * HD] + dot(cots[...], w_cots[: 2 * HD, :], NT)
        packed = 0.0
        for at in range(8):
            half, place = at // 4, at % 4
            if place < 3:
                block = front[:, (3 * half + place) * HD : (3 * half + place + 1) * HD]
            else:
                block = back[:, half * HD : (half + 1) * HD]
            high = block.astype(BF16)
            out[:, at * HD : (at + 1) * HD] = high
            if half == 0:
                packed += low_code(block, high.astype(F32), 4) * 4.0**place
        out[:, 8 * HD : 9 * HD] = packed.astype(BF16)

    @pl.when(role[0] == 1)
    def _():
        columns = w_rows.shape[1]
        out[:, :columns] = (front_a[...] + dot(rows[...], w_rows[...], NN)).astype(BF16)
        out[:, columns:] = (back_a[...] + dot(cots[...], w_cots[...], NT)).astype(BF16)


def attention_kernel(whole, out):
    blocks = []
    for pair in range(4):
        codes = split_codes(whole[:, (8 + pair) * HD : (9 + pair) * HD].astype(F32), 16, 2)
        for at in range(2):
            place = 2 * pair + at
            high = whole[:, place * HD : (place + 1) * HD].astype(F32)
            blocks.append(with_code(high, codes[at], 16))
    q, k, v, cot, tq, tk, tv, cot_tan = blocks
    mixed, q_tan, k_tan, v_tan = attention(q, k, v, tq, tk, tv, cot, cot_tan)
    for at, part in enumerate((q_tan, k_tan, v_tan, mixed)):
        out[:, at * HD : (at + 1) * HD] = part.astype(BF16)
    out[:, 4 * HD :] = jnp.zeros((out.shape[0], out.shape[1] - 4 * HD), BF16)


def products_kernel(role, lows, rows, cots, *refs):
    qkv_out, out_out, up_out, down_out, qkv, out, up, down, sems = refs[-9:]

    def write(at, pair):
        copy = pltpu.make_async_copy(*pair, sems.at[at])
        copy.start()
        return copy

    @pl.when(role[0] == 0)
    def _():
        for at in range(3):
            qkv[at] = dot(rows[...], lows[:, at * HD : (at + 1) * HD], TN).astype(BF16)
        qkv_copy = write(0, (qkv, qkv_out))
        out[...] = dot(lows[:, 3 * HD : 4 * HD], cots[...], TN).astype(BF16)
        out_copy = write(1, (out, out_out))
        qkv_copy.wait()
        out_copy.wait()

    @pl.when(role[0] == 1)
    def _():
        hidden = down.shape[0]
        up[...] = dot(rows[...], lows[:, hidden:], TN).astype(BF16)
        up_copy = write(0, (up, up_out))
        down[...] = dot(lows[:, :hidden], cots[...], TN).astype(BF16)
        down_copy = write(1, (down, down_out))
        up_copy.wait()
        down_copy.wait()


def hidden_pair(pre, cot_in):
    result, pull = jax.vjp(jax.nn.gelu, pre)
    return (result, pull(cot_in)[0])


def body(patches, cotangent, w_qkv, w_out, w_up, w_down, dir_qkv, dir_out, dir_up, dir_down):
    wide = lax.axis_size("mx")
    long = lax.axis_size("my")
    chips = wide // 2
    core = lax.rem(lax.axis_index("mx"), 2)
    ring = [[chip * 2 + c for chip in range(chips)] for c in range(2)]
    swap = [(i, i ^ 1) for i in range(wide)]
    width = w_qkv.shape[0]
    hidden = w_up.shape[1]
    count = patches.shape[0] * long
    share = count // chips

    own_rows = patches.shape[0]
    copy_shape = (long, 2, own_rows, width)
    copies = jnp.where(
        lax.broadcasted_iota(jnp.int32, copy_shape, 1) == 0,
        jnp.broadcast_to(patches, copy_shape),
        jnp.broadcast_to(cotangent, copy_shape),
    )
    gathered = lax.all_to_all(copies, "my", 0, 0, tiled=True)
    swapped = lax.ppermute(gathered, "mx", swap)

    first = core == 0
    flat = lambda a: [a[:, at] for at in range(3)]
    attn_front = jnp.concatenate(flat(w_qkv) + flat(dir_qkv), axis=1)
    attn_front = jnp.pad(attn_front, ((0, 0), (0, 2 * hidden - 6 * HD)))
    attn_back = jnp.pad(jnp.concatenate([w_out, dir_out]), ((0, 2 * hidden - 2 * HD), (0, 0)))
    hid_front = jnp.concatenate([w_up, dir_up], axis=1)
    hid_back = jnp.concatenate([w_down, dir_down])
    kept = (jnp.where(first, attn_front, hid_front), jnp.where(first, attn_back, hid_back))
    lent = (jnp.where(first, hid_front, attn_front), jnp.where(first, hid_back, attn_back))
    taken = tuple(lax.ppermute(a, "mx", swap) for a in lent)
    anywhere = pl.BlockSpec(memory_space=pl.ANY)

    pick = lambda a, at: a[:, at].reshape(count, width)
    rows, cots = pick(gathered, 0), pick(gathered, 1)
    room = pltpu.CompilerParams(vmem_limit_bytes=24 * 2**20)
    cost = lambda flops, read: pl.CostEstimate(flops=flops, bytes_accessed=read, transcendentals=0)
    sums_cost = cost(8 * count * width * hidden, 0)
    own_front, own_back = pl.pallas_call(
        own_sums_kernel,
        out_shape=(jax.ShapeDtypeStruct((count, 2 * hidden), F32),) * 2,
        in_specs=[VMEM] * 4,
        out_specs=(VMEM,) * 2,
        compiler_params=room,
        cost_estimate=sums_cost,
        name="own_sums",
    )(rows, cots, *kept)
    role = lambda a: a.reshape(1).astype(jnp.int32)
    message = pl.pallas_call(
        sums_kernel,
        out_shape=jax.ShapeDtypeStruct((count, 4 * hidden), BF16),
        in_specs=[SMEM] + [VMEM] * 6,
        out_specs=VMEM,
        compiler_params=room,
        cost_estimate=sums_cost,
        name="sums",
    )(role(core), own_front, own_back, pick(swapped, 0), pick(swapped, 1), *taken)

    def exchange(part):
        part = part.reshape(chips, share, -1)
        return lax.all_to_all(part, "mx", 0, 0, tiled=True, axis_index_groups=ring).astype(F32)

    def spread(reply):
        copies = jnp.broadcast_to(reply.astype(BF16), (chips,) + reply.shape)
        whole = lax.all_to_all(copies, "mx", 0, 0, tiled=True, axis_index_groups=ring)
        return whole.reshape(count, -1)

    def attention_part(message):
        parts = exchange(message[:, : 9 * HD])
        block = lambda at: parts[..., at * HD : (at + 1) * HD]
        codes = split_codes(block(8), 4, 4)
        refined = [with_code(block(at), codes[at], 4) for at in range(4)]
        whole = [jnp.sum(a, axis=0) for a in refined + [block(at) for at in range(4, 8)]]
        highs = [lax.reduce_precision(a, 8, 7) for a in whole]
        lows = [low_code(a, high, 16) for a, high in zip(whole, highs)]
        packed = [lows[at] + 16.0 * lows[at + 1] for at in range(0, 8, 2)]
        return pl.pallas_call(
            attention_kernel,
            out_shape=jax.ShapeDtypeStruct((count, 2 * hidden), BF16),
            in_specs=[VMEM],
            out_specs=VMEM,
            compiler_params=room,
            name="attention",
        )(spread(jnp.concatenate(highs + packed, axis=1)))

    def hidden_part(message):
        whole = jnp.sum(exchange(message), axis=0)
        pre_hidden, tan_hidden, cot_act, tan_act = jnp.split(whole, 4, axis=1)
        hid_tan = jax.jvp(hidden_pair, (pre_hidden, cot_act), (tan_hidden, tan_act))[1]
        return spread(jnp.concatenate(hid_tan, axis=1))

    lows = lax.cond(first, attention_part, hidden_part, message)
    theirs = lax.ppermute(lows, "mx", swap)

    shapes = ((3, width, HD), w_out.shape, w_up.shape, w_down.shape)

    def products(which, part, written, name):
        return pl.pallas_call(
            products_kernel,
            out_shape=tuple(jax.ShapeDtypeStruct(shape, BF16) for shape in shapes),
            in_specs=[SMEM] + [VMEM] * 3 + [anywhere] * len(written),
            out_specs=(anywhere,) * 4,
            scratch_shapes=[pltpu.VMEM(shape, BF16) for shape in shapes]
            + [pltpu.SemaphoreType.DMA((2,))],
            input_output_aliases={4 + at: at for at in range(len(written))},
            compiler_params=room,
            cost_estimate=cost(8 * count * width * hidden, 8 * width * hidden),
            name=name,
        )(role(which), part, rows, cots, *written)

    written = products(core, lows, (), "own_products")
    hvp_qkv, hvp_out, hvp_up, hvp_down = products(1 - core, theirs, written, "other_products")
    return jnp.transpose(hvp_qkv, (1, 0, 2)), hvp_out, hvp_up, hvp_down


def solution(mesh):
    return jax.shard_map(
        body,
        mesh=mesh,
        in_specs=(
            P("my", "mx"),
            P("my", "mx"),
            P("mx", None, "my"),
            P("my", "mx"),
            P("mx", "my"),
            P("my", "mx"),
            P("mx", None, "my"),
            P("my", "mx"),
            P("mx", "my"),
            P("my", "mx"),
        ),
        out_specs=(P("mx", None, "my"), P("my", "mx"), P("mx", "my"), P("my", "mx")),
        check_vma=False,
    )
```

```python
import math

import jax
import jax.numpy as jnp
from jax import lax
from jax.experimental import pallas as pl
from jax.experimental.pallas import tpu as pltpu
from jax.sharding import PartitionSpec as P

HD = 128
F32 = jnp.float32
BF16 = jnp.bfloat16
VMEM = pl.BlockSpec(memory_space=pltpu.VMEM)
SMEM = pl.BlockSpec(memory_space=pltpu.SMEM)

NN = ((1,), (0,))
NT = ((1,), (1,))
TN = ((0,), (0,))


def dot(left, right, dims):
    return lax.dot_general(left, right, (dims, ((), ())), preferred_element_type=F32)


def halves(x):
    high = x.astype(BF16)
    return high, (x - high.astype(F32)).astype(BF16)


def product(pairs, dims):
    left = [part for (high, low), _ in pairs for part in (high, high, low)]
    right = [part for _, (high, low) in pairs for part in (high, low, high)]
    return dot(
        jnp.concatenate(left, axis=dims[0][0]), jnp.concatenate(right, axis=dims[1][0]), dims
    )


def low_code(x, high, levels):
    rest = (x - high) / jnp.where(high == 0.0, 1.0, high)
    return jnp.clip(jnp.floor((rest * 256.0 + 1.0) * (levels / 2)), 0.0, levels - 1.0)


def with_code(high, code, levels):
    return high + high * (((code + 0.5) * (2 / levels) - 1.0) / 256.0)


def split_codes(packed, levels, number):
    codes = []
    for place in range(number - 1, 0, -1):
        codes.insert(0, jnp.floor(packed / float(levels) ** place))
        packed = packed - float(levels) ** place * codes[0]
    return [packed] + codes


def mean(x):
    return jnp.mean(x, axis=-1, keepdims=True)


def total(x):
    return jnp.sum(x, axis=-1, keepdims=True)


def centre(x):
    return x - mean(x)


def normalize(x, x_tan):
    centred = centre(x)
    inverse = lax.rsqrt(mean(centred * centred) + 1e-06)
    y = centred * inverse
    shift = mean(y * x_tan)
    return y, (centre(x_tan) - y * shift) * inverse, inverse, shift


def normalize_back(y, y_tan, inverse, shift, cot, cot_tan):
    along = mean(y * cot)
    back = (centre(cot) - y * along) * inverse
    along_tan = mean(y_tan * cot) + mean(y * cot_tan)
    return (centre(cot_tan) - y_tan * along - y * along_tan - back * shift) * inverse


def attention(q, k, v, tq, tk, tv, cot, cot_tan):
    scale = 1.0 / math.sqrt(HD)
    qn, dqn, q_inverse, q_shift = normalize(q, tq)
    kn, dkn, k_inverse, k_shift = normalize(k, tk)
    qs, dqs, ks, dks = halves(qn * scale), halves(dqn * scale), halves(kn), halves(dkn)
    vs, dvs, cs, dcs = halves(v), halves(tv), halves(cot), halves(cot_tan)
    raised = jnp.exp(product([(qs, ks)], NT))
    probs = raised / total(raised)
    score_tan = product([(dqs, ks), (qs, dks)], NT)
    probs_tan = probs * (score_tan - total(probs * score_tan))
    ps, dps = halves(probs), halves(probs_tan)
    mixed_tan = product([(dps, vs), (ps, dvs)], NN)
    v_tan = product([(dps, cs), (ps, dcs)], TN)
    cot_probs = product([(cs, vs)], NT)
    cot_probs_tan = product([(dcs, vs), (cs, dvs)], NT)
    away = cot_probs - total(probs * cot_probs)
    away_tan = cot_probs_tan - total(probs_tan * cot_probs + probs * cot_probs_tan)
    ss, dss = halves(probs * away), halves(probs_tan * away + probs * away_tan)
    q_cot = scale * product([(ss, ks)], NN)
    q_cot_tan = scale * product([(dss, ks), (ss, dks)], NN)
    k_cot = product([(ss, qs)], TN)
    k_cot_tan = product([(dss, qs), (ss, dqs)], TN)
    q_tan = normalize_back(qn, dqn, q_inverse, q_shift, q_cot, q_cot_tan)
    k_tan = normalize_back(kn, dkn, k_inverse, k_shift, k_cot, k_cot_tan)
    return mixed_tan, q_tan, k_tan, v_tan


def own_sums_kernel(rows, cots, w_rows, w_cots, front, back):
    front[...] = dot(rows[...], w_rows[...], NN)
    back[...] = dot(cots[...], w_cots[...], NT)


def sums_kernel(role, front_a, back_a, rows, cots, far_rows, far_cots, out, w_rows, w_cots, sems):
    columns = w_rows.shape[1]

    def bring(pairs):
        copies = [pltpu.make_async_copy(*pair, sems.at[at]) for at, pair in enumerate(pairs)]
        for copy in copies:
            copy.start()
        return copies

    @pl.when(role[0] == 0)
    def _():
        heads = slice(0, 6 * HD)
        outs = slice(0, 2 * HD)
        for copy in bring(
            [
                (far_rows.at[:, heads], w_rows.at[:, heads]),
                (far_cots.at[outs, :], w_cots.at[outs, :]),
            ]
        ):
            copy.wait()
        front = front_a[:, heads] + dot(rows[...], w_rows[:, heads], NN)
        back = back_a[:, outs] + dot(cots[...], w_cots[outs, :], NT)
        packed = 0.0
        for at in range(8):
            half, place = at // 4, at % 4
            if place < 3:
                block = front[:, (3 * half + place) * HD : (3 * half + place + 1) * HD]
            else:
                block = back[:, half * HD : (half + 1) * HD]
            high = block.astype(BF16)
            out[:, at * HD : (at + 1) * HD] = high
            if half == 0:
                packed += low_code(block, high.astype(F32), 4) * 4.0**place
        out[:, 8 * HD : 9 * HD] = packed.astype(BF16)

    @pl.when(role[0] == 1)
    def _():
        halves_of = [slice(0, columns // 2), slice(columns // 2, columns)]
        copies = bring(
            [(far_cots.at[at, :], w_cots.at[at, :]) for at in halves_of] + [(far_rows, w_rows)]
        )
        for copy, at in zip(copies, halves_of):
            copy.wait()
            sums = back_a[:, at] + dot(cots[...], w_cots[at, :], NT)
            out[:, columns + at.start : columns + at.stop] = sums.astype(BF16)
        copies[2].wait()
        out[:, :columns] = (front_a[...] + dot(rows[...], w_rows[...], NN)).astype(BF16)


def attention_kernel(whole, out):
    blocks = []
    for pair in range(4):
        codes = split_codes(whole[:, (8 + pair) * HD : (9 + pair) * HD].astype(F32), 16, 2)
        for at in range(2):
            place = 2 * pair + at
            high = whole[:, place * HD : (place + 1) * HD].astype(F32)
            blocks.append(with_code(high, codes[at], 16))
    q, k, v, cot, tq, tk, tv, cot_tan = blocks
    mixed, q_tan, k_tan, v_tan = attention(q, k, v, tq, tk, tv, cot, cot_tan)
    for at, part in enumerate((q_tan, k_tan, v_tan, mixed)):
        out[:, at * HD : (at + 1) * HD] = part.astype(BF16)
    out[:, 4 * HD :] = jnp.zeros((out.shape[0], out.shape[1] - 4 * HD), BF16)


def products_kernel(role, lows, rows, cots, *refs):
    qkv_out, out_out, up_out, down_out, qkv, out, up, down, sems = refs[-9:]

    def write(at, pair):
        copy = pltpu.make_async_copy(*pair, sems.at[at])
        copy.start()
        return copy

    @pl.when(role[0] == 0)
    def _():
        for at in range(3):
            qkv[at] = dot(rows[...], lows[:, at * HD : (at + 1) * HD], TN).astype(BF16)
        qkv_copy = write(0, (qkv, qkv_out))
        out[...] = dot(lows[:, 3 * HD : 4 * HD], cots[...], TN).astype(BF16)
        out_copy = write(1, (out, out_out))
        qkv_copy.wait()
        out_copy.wait()

    @pl.when(role[0] == 1)
    def _():
        hidden = down.shape[0]
        up[...] = dot(rows[...], lows[:, hidden:], TN).astype(BF16)
        up_copy = write(0, (up, up_out))
        down[...] = dot(lows[:, :hidden], cots[...], TN).astype(BF16)
        down_copy = write(1, (down, down_out))
        up_copy.wait()
        down_copy.wait()


def hidden_pair(pre, cot_in):
    result, pull = jax.vjp(jax.nn.gelu, pre)
    return (result, pull(cot_in)[0])


def body(patches, cotangent, w_qkv, w_out, w_up, w_down, dir_qkv, dir_out, dir_up, dir_down):
    wide = lax.axis_size("mx")
    long = lax.axis_size("my")
    chips = wide // 2
    core = lax.rem(lax.axis_index("mx"), 2)
    ring = [[chip * 2 + c for chip in range(chips)] for c in range(2)]
    swap = [(i, i ^ 1) for i in range(wide)]
    width = w_qkv.shape[0]
    hidden = w_up.shape[1]
    count = patches.shape[0] * long
    share = count // chips

    own_rows = patches.shape[0]
    copy_shape = (long, 2, own_rows, width)
    copies = jnp.where(
        lax.broadcasted_iota(jnp.int32, copy_shape, 1) == 0,
        jnp.broadcast_to(patches, copy_shape),
        jnp.broadcast_to(cotangent, copy_shape),
    )
    gathered = lax.all_to_all(copies, "my", 0, 0, tiled=True)
    swapped = lax.ppermute(gathered, "mx", swap)

    first = core == 0
    flat = lambda a: [a[:, at] for at in range(3)]
    attn_front = jnp.concatenate(flat(w_qkv) + flat(dir_qkv), axis=1)
    attn_front = jnp.pad(attn_front, ((0, 0), (0, 2 * hidden - 6 * HD)))
    attn_back = jnp.pad(jnp.concatenate([w_out, dir_out]), ((0, 2 * hidden - 2 * HD), (0, 0)))
    hid_front = jnp.concatenate([w_up, dir_up], axis=1)
    hid_back = jnp.concatenate([w_down, dir_down])
    kept = (jnp.where(first, attn_front, hid_front), jnp.where(first, attn_back, hid_back))
    lent = (jnp.where(first, hid_front, attn_front), jnp.where(first, hid_back, attn_back))
    taken = tuple(lax.ppermute(a, "mx", swap) for a in lent)
    anywhere = pl.BlockSpec(memory_space=pl.ANY)

    pick = lambda a, at: a[:, at].reshape(count, width)
    rows, cots = pick(gathered, 0), pick(gathered, 1)
    room = pltpu.CompilerParams(vmem_limit_bytes=24 * 2**20)
    cost = lambda flops, read: pl.CostEstimate(flops=flops, bytes_accessed=read, transcendentals=0)
    sums_cost = cost(8 * count * width * hidden, 0)
    own_front, own_back = pl.pallas_call(
        own_sums_kernel,
        out_shape=(jax.ShapeDtypeStruct((count, 2 * hidden), F32),) * 2,
        in_specs=[VMEM] * 4,
        out_specs=(VMEM,) * 2,
        compiler_params=room,
        cost_estimate=sums_cost,
        name="own_sums",
    )(rows, cots, *kept)
    role = lambda a: a.reshape(1).astype(jnp.int32)
    message = pl.pallas_call(
        sums_kernel,
        out_shape=jax.ShapeDtypeStruct((count, 4 * hidden), BF16),
        in_specs=[SMEM] + [VMEM] * 4 + [anywhere] * 2,
        out_specs=VMEM,
        scratch_shapes=[pltpu.VMEM(a.shape, a.dtype) for a in taken]
        + [pltpu.SemaphoreType.DMA((3,))],
        compiler_params=room,
        cost_estimate=sums_cost,
        name="sums",
    )(role(core), own_front, own_back, pick(swapped, 0), pick(swapped, 1), *taken)

    def exchange(part):
        part = part.reshape(chips, share, -1)
        return lax.all_to_all(part, "mx", 0, 0, tiled=True, axis_index_groups=ring).astype(F32)

    def spread(reply):
        copies = jnp.broadcast_to(reply.astype(BF16), (chips,) + reply.shape)
        whole = lax.all_to_all(copies, "mx", 0, 0, tiled=True, axis_index_groups=ring)
        return whole.reshape(count, -1)

    def attention_part(message):
        parts = exchange(message[:, : 9 * HD])
        block = lambda at: parts[..., at * HD : (at + 1) * HD]
        codes = split_codes(block(8), 4, 4)
        refined = [with_code(block(at), codes[at], 4) for at in range(4)]
        whole = [jnp.sum(a, axis=0) for a in refined + [block(at) for at in range(4, 8)]]
        highs = [lax.reduce_precision(a, 8, 7) for a in whole]
        lows = [low_code(a, high, 16) for a, high in zip(whole, highs)]
        packed = [lows[at] + 16.0 * lows[at + 1] for at in range(0, 8, 2)]
        return pl.pallas_call(
            attention_kernel,
            out_shape=jax.ShapeDtypeStruct((count, 2 * hidden), BF16),
            in_specs=[VMEM],
            out_specs=VMEM,
            compiler_params=room,
            name="attention",
        )(spread(jnp.concatenate(highs + packed, axis=1)))

    def hidden_part(message):
        whole = jnp.sum(exchange(message), axis=0)
        pre_hidden, tan_hidden, cot_act, tan_act = jnp.split(whole, 4, axis=1)
        hid_tan = jax.jvp(hidden_pair, (pre_hidden, cot_act), (tan_hidden, tan_act))[1]
        return spread(jnp.concatenate(hid_tan, axis=1))

    lows = lax.cond(first, attention_part, hidden_part, message)
    theirs = lax.ppermute(lows, "mx", swap)

    shapes = ((3, width, HD), w_out.shape, w_up.shape, w_down.shape)

    def products(which, part, written, name):
        return pl.pallas_call(
            products_kernel,
            out_shape=tuple(jax.ShapeDtypeStruct(shape, BF16) for shape in shapes),
            in_specs=[SMEM] + [VMEM] * 3 + [anywhere] * len(written),
            out_specs=(anywhere,) * 4,
            scratch_shapes=[pltpu.VMEM(shape, BF16) for shape in shapes]
            + [pltpu.SemaphoreType.DMA((2,))],
            input_output_aliases={4 + at: at for at in range(len(written))},
            compiler_params=room,
            cost_estimate=cost(8 * count * width * hidden, 8 * width * hidden),
            name=name,
        )(role(which), part, rows, cots, *written)

    written = products(core, lows, (), "own_products")
    hvp_qkv, hvp_out, hvp_up, hvp_down = products(1 - core, theirs, written, "other_products")
    return jnp.transpose(hvp_qkv, (1, 0, 2)), hvp_out, hvp_up, hvp_down


def solution(mesh):
    return jax.shard_map(
        body,
        mesh=mesh,
        in_specs=(
            P("my", "mx"),
            P("my", "mx"),
            P("mx", None, "my"),
            P("my", "mx"),
            P("mx", "my"),
            P("my", "mx"),
            P("mx", None, "my"),
            P("my", "mx"),
            P("mx", "my"),
            P("my", "mx"),
        ),
        out_specs=(P("mx", None, "my"), P("my", "mx"), P("mx", "my"), P("my", "mx")),
        check_vma=False,
    )
```
